32 devices in a mesh: pole: 2 (over y), row: 16 (over z, x, core).
Axes of the slice: x: 2, y: 2, z: 4, core: 2. Of those that a mesh axis runs over, the one named last changes fastest.
Arguments:
- root_inverse: bfloat16 [6144, 3072], P(('pole', 'row')), parts along dimension 0, may hold values from -6 to 6
- structure: int32 [16, 8], P('row'), may hold values from 0 to 11, all different within a row
- lower_panel: bfloat16 [32, 2048, 1024], P(('pole', 'row')), parts along dimension 0, may hold values from -0.125 to 0.125
- diag_inverse: bfloat16 [32, 1024, 1024], P(('pole', 'row')), parts along dimension 0, may hold values from -6 to 6
Outputs:
- inverse_off: bfloat16 [32, 2048, 1024], P(('pole', 'row')), parts along dimension 0
- inverse_diag: bfloat16 [32, 1024, 1024], P(('pole', 'row')), parts along dimension 0
The draws below stay inside these ranges and needn't reach their ends.
There are 2 independent parts, one for each index of `pole`. The reference program is written for one: setup_inputs(seed, part) draws one part's arguments, and reference() takes and returns one part's arrays. A program takes and returns all parts, laid end to end along the dimension named above; an argument that names none is the same for every part. Nothing has to cross between parts.
Inputs may be any that keep to these rules, and one draw needn't show every extreme that they name: `structure`: the 8 root blocks named by one child are distinct; every root block is named by some child.
All inputs are finite; a program needn't handle non-finite values.
Results may differ from the reference program's by a relative error of at most 0.0041.
Values may be sent and summed in bfloat16 or wider, within the bound.
A program may use at most 128 MiB of HBM per device.

```python
import jax
import jax.numpy as jnp
from jax import lax

B = 256
RB = 12
S = 8
CW = 4
NK = 16


def level_of(key, shape, shards, low, top_value):
    factor_of = 1.0
    for dim, shards_of in shards:
        draws = jax.random.uniform(jax.random.fold_in(jax.random.fold_in(key, 6), dim), (shards_of,), jnp.float32, low / len(shards), top_value / len(shards))
        factor_of = factor_of * jnp.repeat(jnp.exp(draws), shape[dim] // shards_of).reshape((-1,) + (1,) * (len(shape) - 1 - dim))
    return factor_of


def picks_of(key, rows, count, top, lift):
    ranking = jax.random.permutation(jax.random.fold_in(key, 1), count)
    boost = ranking
    for power in range(3):
        boost = boost * boost // count
    boost = boost * lift // count
    lots = jax.random.randint(jax.random.fold_in(key, 2), (rows, count), 0, 4096) + boost
    fixed_rows = jax.random.permutation(jax.random.fold_in(key, 3), rows)[jnp.arange(count) % rows]
    lots = jnp.where(jnp.arange(rows)[:, None] == fixed_rows[None, :], 1 << 14, lots)
    score = lots * count + jnp.arange(count)
    return lax.top_k(score.astype(jnp.int32), top)[1].astype(jnp.int32)


def noise(key, shape, spread, limit, cuts=(), held_as=jnp.bfloat16):
    array = spread * jax.random.normal(key, shape, jnp.float32)
    if cuts:
        array = array * level_of(key, shape, cuts, -0.22, 0.18)
    return jnp.clip(array, -limit, limit).astype(held_as)


def setup_inputs(seed: int = 0, part: int = 0) -> dict:
    streams_of = jax.random.split(jax.random.key(seed), 5)
    part_keys = jax.random.split(jax.random.fold_in(streams_of[4], part), 5)
    root_inverse = noise(part_keys[0], (RB * B, RB * B), 1.0, 6.0, ((0, 16),))
    structure = picks_of(streams_of[1], NK, RB, S, 0)
    lower_panel = noise(part_keys[2], (NK, S * B, CW * B), (S * B) ** -0.5, 0.125, ((0, 16),))
    diag_inverse = noise(part_keys[3], (NK, CW * B, CW * B), 1.0, 6.0, ((0, 16),))
    return {"root_inverse": root_inverse, "structure": structure, "lower_panel": lower_panel, "diag_inverse": diag_inverse}


def one_child(blocked, struct_ids, lower, diag_inv):
    picked_rows = jnp.take(blocked, struct_ids, axis=0)
    root_block = jnp.take(picked_rows, struct_ids, axis=2).reshape(S * B, S * B)
    product = jnp.dot(root_block, lower, preferred_element_type=jnp.float32)
    off_block = (-product).astype(jnp.bfloat16)
    update = jnp.dot(lower.T, off_block, preferred_element_type=jnp.float32)
    diag_block = (diag_inv.astype(jnp.float32) - update).astype(jnp.bfloat16)
    return off_block, diag_block


def reference(root_inverse, structure, lower_panel, diag_inverse):
    blocked = root_inverse.reshape(RB, B, RB, B)

    def apply_child(item):
        return one_child(blocked, item[0], item[1], item[2])

    inverse_off, inverse_diag = lax.map(apply_child, (structure, lower_panel, diag_inverse))
    return inverse_off, inverse_diag
```

```python
import jax
import jax.numpy as jnp
from jax import lax
from jax.experimental import pallas as pl
from jax.experimental.pallas import tpu as pltpu
from jax.sharding import PartitionSpec as P

B = 256
RB = 12
S = 8
MESH = pl.DeviceIdType.MESH
Q = 2
SUB = 2 * Q
TILE = 256
STRIP = 16


def pick(index, values):
    out = values[-1]
    for i in range(len(values) - 2, -1, -1):
        out = jnp.where(index == i, values[i], out)
    return out


def gather_kernel(
    root, struct, lower, diag_in, off_out, diag_out,
    gbuf, lv, lfull, acc, offv, dv, lt,
    recv, send_sib, send_x, send_zp, send_zm, own_sem, in_sem, off_sem, out_sem,
):
    piece = gbuf.shape[2]
    half = piece * Q
    pole = lax.axis_index("pole")
    me = lax.axis_index("row")
    core = me % 2
    x = (me // 2) % 2
    z = me // 4
    low = z < 2
    end = jnp.logical_or(z == 0, z == 3)
    mid = jnp.logical_not(end)

    def zn(i):
        return jnp.where(low, i, 3 - i)

    ia = jnp.where(end, 0, 1)
    za, zb, z2, z3 = zn(ia), zn(1 - ia), zn(2), zn(3)
    zsym = {"a": za, "b": zb, "2": z2, "3": z3}

    def device(zz, xx, cc):
        return (pole, (zz * 2 + xx) * 2 + cc)

    peers = {
        "sib": (device(z, x, 1 - core), send_sib),
        "x": (device(z, 1 - x, core), send_x),
        "zp": (device(zb, x, core), send_zp),
        "zm": (device(z2, x, core), send_zm),
    }

    def unit_of(zz, xx, h):
        return (zz * 2 + xx) * 2 + h

    sent = []

    def copy_of(direction, name, other, c, from_input=False):
        peer, sems = peers[direction]
        h, q = c // Q, c % Q
        unit = unit_of(zsym[name], 1 - x if other else x, h)
        sub = core * Q + q
        dst = gbuf.at[unit, sub]
        src = root.at[h, q] if from_input else dst
        return pltpu.make_async_remote_copy(
            src_ref=src, dst_ref=dst,
            send_sem=sems.at[unit, q], recv_sem=recv.at[unit, sub],
            device_id=peer, device_id_type=MESH,
        )

    def forward(when, direction, name, other, c, from_input=False):
        sent.append((when, direction, name, other, c, from_input))
        copy_of(direction, name, other, c, from_input).start()

    def arrive(name, other, c):
        copy_of("sib", name, other, c).wait_recv()

    own_copies = [
        pltpu.make_async_copy(
            root.at[c // Q, c % Q],
            gbuf.at[unit_of(za, x, c // Q), core * Q + c % Q],
            own_sem.at[c],
        )
        for c in range(2 * Q)
    ]
    l_copy = pltpu.make_async_copy(lower, lv, in_sem.at[0])
    d_copy = pltpu.make_async_copy(diag_in, dv, in_sem.at[1])

    barrier = pltpu.get_barrier_semaphore()
    for direction in ("sib", "x", "zp"):
        pl.semaphore_signal(barrier, inc=1, device_id=peers[direction][0], device_id_type=MESH)

    @pl.when(mid)
    def _():
        pl.semaphore_signal(barrier, inc=1, device_id=peers["zm"][0], device_id_type=MESH)

    l_copy.start()
    for copy in own_copies:
        copy.start()
    d_copy.start()
    pl.semaphore_wait(barrier, jnp.where(mid, 4, 3))

    quarters = range(2 * Q)
    for c in quarters:
        forward(None, "zp", "a", False, c, True)
        forward(None, "x", "a", False, c, True)
        forward(None, "sib", "a", False, c, True)

    @pl.when(mid)
    def _():
        for c in quarters:
            forward("mid", "zm", "a", False, c, True)

    l_copy.wait()

    @pl.loop(0, RB)
    def _(r):
        weights = [jnp.where(struct[0, s] == r, 1.0, 0.0) for s in range(S)]

        @pl.loop(0, B // STRIP)
        def _(t):
            start = pl.multiple_of(t * STRIP, STRIP)
            total = jnp.zeros((STRIP, lv.shape[1]), jnp.float32)
            for s in range(S):
                total += weights[s] * lv[pl.ds(s * B + start, STRIP), :].astype(jnp.float32)
            to = pl.multiple_of(r * B + t * STRIP, STRIP)
            lfull[pl.ds(to, STRIP), :] = total.astype(jnp.bfloat16)

    d_copy.wait()
    acc[...] = dv[...].astype(jnp.float32)
    for copy in own_copies:
        copy.wait()

    def on(flag, actions):
        @pl.when(end if flag == "end" else mid)
        def _():
            actions()

    def step1(c):
        arrive("b", False, c)
        if c < Q:
            forward(None, "x", "b", False, c)
        forward(None, "sib", "b", False, c)
        on("mid", lambda: forward("mid", "zm", "b", False, c))
        arrive("a", True, c)
        forward(None, "sib", "a", True, c)
        if c >= Q:
            on("end", lambda: forward("end", "zp", "a", True, c))

        def middle():
            arrive("2", False, c)
            forward("mid", "zp", "2", False, c)
            forward("mid", "x", "2", False, c)
            forward("mid", "sib", "2", False, c)

        on("mid", middle)

    def step_b_first(c):
        arrive("b", True, c)
        forward(None, "sib", "b", True, c)

    def end_own(name, c):
        def actions():
            arrive(name, False, c)
            forward("end", "x", name, False, c)
            forward("end", "sib", name, False, c)

        on("end", actions)

    def mid_three(c):
        def actions():
            arrive("3", False, c)
            forward("mid", "zp", "3", False, c)
            forward("mid", "x", "3", False, c)
            forward("mid", "sib", "3", False, c)

        on("mid", actions)

    def mid_last(c):
        def actions():
            arrive("b", True, c)
            forward("mid", "sib", "b", True, c)
            forward("mid", "zp", "a", True, c)

        on("mid", actions)

    def end_last(c):
        def actions():
            arrive("b", True, c)
            forward("end", "sib", "b", True, c)

        on("end", actions)

    def other(name, c):
        arrive(name, True, c)
        forward(None, "sib", name, True, c)

    def phase(k):
        first, second = range(Q), range(Q, 2 * Q)
        if k == 1:
            for c in first:
                step1(c)
        elif k == 2:
            for c in second:
                step1(c)
        elif k == 3:
            for c in first:
                step_b_first(c)
                end_own("2", c)
                mid_three(c)
        elif k == 4:
            for c in first:
                other("2", c)
                end_own("2", c + Q)
                mid_three(c + Q)
        elif k == 5:
            for c in second:
                mid_last(c)
            for c in first:
                other("2", c + Q)
                end_own("3", c)
        elif k == 6:
            for c in first:
                other("3", c)
                end_own("3", c + Q)
        elif k == 7:
            for c in second:
                other("3", c)
                end_last(c)

    table = [
        ("a", 0, 0), ("a", 0, 1),
        ("b", 0, 0), ("a", 1, 0),
        ("b", 0, 1), ("a", 1, 1),
        ("b", 1, 0), ("2", 0, 0),
        ("2", 0, 1), ("2", 1, 0),
        ("2", 1, 1), ("3", 0, 0),
        ("3", 0, 1), ("3", 1, 0),
        ("3", 1, 1), ("b", 1, 1),
    ]

    def off_copy(unit, p):
        return pltpu.make_async_copy(
            offv.at[unit, p], off_out.at[unit // 2, p, unit % 2], off_sem.at[unit, p]
        )

    @pl.loop(0, 8)
    def _(g):
        for k in range(1, 8):
            pl.when(g == k)(lambda k=k: phase(k))

        @pl.loop(0, 2)
        def _(j):
            i = g * 2 + j
            chip_z = pick(i, [zsym[name] for name, _, _ in table])
            chip_x = pick(i, [1 - x if o else x for _, o, _ in table])
            h = pick(i, [jnp.int32(hh) for _, _, hh in table])
            unit = unit_of(chip_z, chip_x, h)
            for q in range(Q):
                sub = (1 - core) * Q + q
                pltpu.make_async_copy(
                    gbuf.at[unit, sub], gbuf.at[unit, sub], recv.at[unit, sub]
                ).wait()
            chip = unit // 2
            rows = []
            for p in range(2):
                start = pl.multiple_of(chip * (4 * half) + p * 2 * half + h * half, half)
                rows.append(lfull[pl.ds(start, half), :])
            lt[...] = jnp.concatenate(rows, axis=0).T

            @pl.loop(0, acc.shape[1] // TILE)
            def _(n):
                cols = pl.ds(pl.multiple_of(n * TILE, TILE), TILE)
                left = gbuf[unit].reshape(2 * half, gbuf.shape[3])
                part = jnp.dot(left, lfull[:, cols], preferred_element_type=jnp.float32)
                off = (-part).astype(jnp.bfloat16)
                offv[unit, 0, :, cols] = off[:half]
                offv[unit, 1, :, cols] = off[half:]
                acc[:, cols] -= jnp.dot(lt[...], off, preferred_element_type=jnp.float32)

            for p in range(2):
                off_copy(unit, p).start()

    dv[...] = acc[...].astype(jnp.bfloat16)
    out_copy = pltpu.make_async_copy(dv, diag_out, out_sem.at[0])
    out_copy.start()

    for flag in (None, "mid", "end"):
        def drain(flag=flag):
            for when, direction, name, o, c, from_input in sent:
                if when == flag:
                    copy_of(direction, name, o, c, from_input).wait_send()

        if flag is None:
            drain()
        else:
            on(flag, drain)

    @pl.loop(0, 16)
    def _(unit):
        for p in range(2):
            off_copy(unit, p).wait()

    out_copy.wait()


def pick_kernel(struct, off_ref, diag_ref, off_out, diag_out):
    off_out[...] = off_ref[...]
    diag_out[...] = diag_ref[...]


def fast(root_inverse, structure, lower_panel, diag_inverse):
    rows, width = root_inverse.shape
    depth, cols = lower_panel.shape[1:]
    piece = rows // (2 * Q)
    half = rows // 2
    chips = lax.axis_size("row") // 2
    units = 2 * chips
    bf16 = jnp.bfloat16
    dma = pltpu.SemaphoreType.DMA
    any_space = pl.BlockSpec(memory_space=pl.ANY)
    off_full, diag = pl.pallas_call(
        gather_kernel,
        out_shape=(
            jax.ShapeDtypeStruct((chips, 2, 2, half, cols), bf16),
            jax.ShapeDtypeStruct((cols, cols), bf16),
        ),
        in_specs=[any_space, pl.BlockSpec(memory_space=pltpu.SMEM), any_space, any_space],
        out_specs=(any_space, any_space),
        scratch_shapes=[
            pltpu.VMEM((units, SUB, piece, width), bf16),
            pltpu.VMEM((depth, cols), bf16),
            pltpu.VMEM((width, cols), bf16),
            pltpu.VMEM((cols, cols), jnp.float32),
            pltpu.VMEM((units, 2, half, cols), bf16),
            pltpu.VMEM((cols, cols), bf16),
            pltpu.VMEM((cols, 2 * half), bf16),
            dma((units, SUB)),
            dma((units, Q)),
            dma((units, Q)),
            dma((units, Q)),
            dma((units, Q)),
            dma((2 * Q,)),
            dma((2,)),
            dma((units, 2)),
            dma((1,)),
        ],
        compiler_params=pltpu.CompilerParams(
            collective_id=0, has_side_effects=True, vmem_limit_bytes=56 * 1024 * 1024
        ),
        cost_estimate=pl.CostEstimate(
            flops=2 * width * cols * (width + cols), bytes_accessed=20 * 2**20, transcendentals=0
        ),
    )(root_inverse.reshape(2, Q, piece, width), structure, lower_panel[0], diag_inverse[0])
    off_full = off_full.reshape(RB, B, cols)
    strip = cols // S
    off, diag = pl.pallas_call(
        pick_kernel,
        grid_spec=pltpu.PrefetchScalarGridSpec(
            num_scalar_prefetch=1,
            grid=(S,),
            in_specs=[
                pl.BlockSpec((1, B, cols), lambda s, st: (st[s], 0, 0)),
                pl.BlockSpec((strip, cols), lambda s, st: (s, 0)),
            ],
            out_specs=[
                pl.BlockSpec((1, B, cols), lambda s, st: (s, 0, 0)),
                pl.BlockSpec((strip, cols), lambda s, st: (s, 0)),
            ],
        ),
        out_shape=(
            jax.ShapeDtypeStruct((S, B, cols), bf16),
            jax.ShapeDtypeStruct((cols, cols), bf16),
        ),
    )(structure[0], off_full, diag)
    return off.reshape(1, depth, cols), diag[None]


def general(root_inverse, structure, lower_panel, diag_inverse):
    whole = lax.all_gather(root_inverse, "row", axis=0, tiled=True).reshape(RB, B, RB, B)
    offs, diags = [], []
    for child in range(structure.shape[0]):
        picked = jnp.take(whole, structure[child], axis=0)
        block = jnp.take(picked, structure[child], axis=2).reshape(S * B, S * B)
        lower = lower_panel[child]
        off = (-jnp.dot(block, lower, preferred_element_type=jnp.float32)).astype(jnp.bfloat16)
        update = lax.dot_general(
            lower, off, (((0,), (0,)), ((), ())), preferred_element_type=jnp.float32
        )
        offs.append(off)
        diags.append((diag_inverse[child].astype(jnp.float32) - update).astype(jnp.bfloat16))
    return jnp.stack(offs), jnp.stack(diags)


def solution(mesh):
    per_device = fast if mesh.shape["row"] == 16 else general
    in_specs = (
        P(("pole", "row"), None),
        P("row", None),
        P(("pole", "row"), None, None),
        P(("pole", "row"), None, None),
    )
    out_specs = (P(("pole", "row"), None, None), P(("pole", "row"), None, None))
    return jax.shard_map(
        per_device, mesh=mesh, in_specs=in_specs, out_specs=out_specs, check_vma=False
    )
```

```python
import jax
import jax.numpy as jnp
from jax import lax
from jax.experimental import pallas as pl
from jax.experimental.pallas import tpu as pltpu
from jax.sharding import PartitionSpec as P

B = 256
RB = 12
S = 8
MESH = pl.DeviceIdType.MESH
Q = 2
SUB = 2 * Q
TILE = 256
STRIP = 16


def pick(index, values):
    out = values[-1]
    for i in range(len(values) - 2, -1, -1):
        out = jnp.where(index == i, values[i], out)
    return out


def gather_kernel(
    root, struct, lower, diag_in, off_out, diag_out,
    gbuf, lv, lfull, acc, offv, dv, lt,
    recv, send_sib, send_x, send_zp, send_zm, own_sem, in_sem, off_sem, out_sem,
):
    piece = gbuf.shape[2]
    half = piece * Q
    pole = lax.axis_index("pole")
    me = lax.axis_index("row")
    core = me % 2
    x = (me // 2) % 2
    z = me // 4
    low = z < 2
    end = jnp.logical_or(z == 0, z == 3)
    mid = jnp.logical_not(end)

    def zn(i):
        return jnp.where(low, i, 3 - i)

    ia = jnp.where(end, 0, 1)
    za, zb, z2, z3 = zn(ia), zn(1 - ia), zn(2), zn(3)
    zsym = {"a": za, "b": zb, "2": z2, "3": z3}

    def device(zz, xx, cc):
        return (pole, (zz * 2 + xx) * 2 + cc)

    peers = {
        "sib": (device(z, x, 1 - core), send_sib),
        "x": (device(z, 1 - x, core), send_x),
        "zp": (device(zb, x, core), send_zp),
        "zm": (device(z2, x, core), send_zm),
    }

    def unit_of(zz, xx, h):
        return (zz * 2 + xx) * 2 + h

    sent = []

    def copy_of(direction, name, other, c, from_input=False):
        peer, sems = peers[direction]
        h, q = c // Q, c % Q
        unit = unit_of(zsym[name], 1 - x if other else x, h)
        sub = core * Q + q
        dst = gbuf.at[unit, sub]
        src = root.at[h, q] if from_input else dst
        return pltpu.make_async_remote_copy(
            src_ref=src, dst_ref=dst,
            send_sem=sems.at[unit, q], recv_sem=recv.at[unit, sub],
            device_id=peer, device_id_type=MESH,
        )

    def forward(when, direction, name, other, c, from_input=False):
        sent.append((when, direction, name, other, c, from_input))
        copy_of(direction, name, other, c, from_input).start()

    def arrive(name, other, c):
        copy_of("sib", name, other, c).wait_recv()

    own_copies = [
        pltpu.make_async_copy(
            root.at[c // Q, c % Q],
            gbuf.at[unit_of(za, x, c // Q), core * Q + c % Q],
            own_sem.at[c],
        )
        for c in range(2 * Q)
    ]
    l_copy = pltpu.make_async_copy(lower, lv, in_sem.at[0])
    d_copy = pltpu.make_async_copy(diag_in, dv, in_sem.at[1])

    barrier = pltpu.get_barrier_semaphore()
    for direction in ("sib", "x", "zp"):
        pl.semaphore_signal(barrier, inc=1, device_id=peers[direction][0], device_id_type=MESH)

    @pl.when(mid)
    def _():
        pl.semaphore_signal(barrier, inc=1, device_id=peers["zm"][0], device_id_type=MESH)

    l_copy.start()
    for copy in own_copies:
        copy.start()
    d_copy.start()
    pl.semaphore_wait(barrier, jnp.where(mid, 4, 3))

    quarters = range(2 * Q)
    for c in quarters:
        forward(None, "zp", "a", False, c, True)
        forward(None, "x", "a", False, c, True)
        forward(None, "sib", "a", False, c, True)

    @pl.when(mid)
    def _():
        for c in quarters:
            forward("mid", "zm", "a", False, c, True)

    l_copy.wait()

    @pl.loop(0, RB)
    def _(r):
        weights = [jnp.where(struct[0, s] == r, 1.0, 0.0) for s in range(S)]

        @pl.loop(0, B // STRIP)
        def _(t):
            start = pl.multiple_of(t * STRIP, STRIP)
            total = jnp.zeros((STRIP, lv.shape[1]), jnp.float32)
            for s in range(S):
                total += weights[s] * lv[pl.ds(s * B + start, STRIP), :].astype(jnp.float32)
            to = pl.multiple_of(r * B + t * STRIP, STRIP)
            lfull[pl.ds(to, STRIP), :] = total.astype(jnp.bfloat16)

    d_copy.wait()
    acc[...] = dv[...].astype(jnp.float32)
    for copy in own_copies:
        copy.wait()

    def on(flag, actions):
        @pl.when(end if flag == "end" else mid)
        def _():
            actions()

    def step1(c):
        arrive("b", False, c)
        if c < Q:
            forward(None, "x", "b", False, c)
        forward(None, "sib", "b", False, c)
        on("mid", lambda: forward("mid", "zm", "b", False, c))
        arrive("a", True, c)
        forward(None, "sib", "a", True, c)
        if c >= Q:
            on("end", lambda: forward("end", "zp", "a", True, c))

        def middle():
            arrive("2", False, c)
            forward("mid", "zp", "2", False, c)
            forward("mid", "x", "2", False, c)
            forward("mid", "sib", "2", False, c)

        on("mid", middle)

    def step_b_first(c):
        arrive("b", True, c)
        forward(None, "sib", "b", True, c)

    def end_own(name, c):
        def actions():
            arrive(name, False, c)
            forward("end", "x", name, False, c)
            forward("end", "sib", name, False, c)

        on("end", actions)

    def mid_three(c):
        def actions():
            arrive("3", False, c)
            forward("mid", "zp", "3", False, c)
            forward("mid", "x", "3", False, c)
            forward("mid", "sib", "3", False, c)

        on("mid", actions)

    def mid_last(c):
        def actions():
            arrive("b", True, c)
            forward("mid", "sib", "b", True, c)
            forward("mid", "zp", "a", True, c)

        on("mid", actions)

    def end_last(c):
        def actions():
            arrive("b", True, c)
            forward("end", "sib", "b", True, c)

        on("end", actions)

    def other(name, c):
        arrive(name, True, c)
        forward(None, "sib", name, True, c)

    def phase(k):
        first, second = range(Q), range(Q, 2 * Q)
        if k == 1:
            for c in first:
                step1(c)
        elif k == 2:
            for c in second:
                step1(c)
        elif k == 3:
            for c in first:
                step_b_first(c)
                end_own("2", c)
                mid_three(c)
        elif k == 4:
            for c in first:
                other("2", c)
                end_own("2", c + Q)
                mid_three(c + Q)
        elif k == 5:
            for c in second:
                mid_last(c)
            for c in first:
                other("2", c + Q)
                end_own("3", c)
        elif k == 6:
            for c in first:
                other("3", c)
                end_own("3", c + Q)

    def last_phase(t):
        step = Q // 2
        for c in range(Q + t * step, Q + (t + 1) * step):
            other("3", c)
            end_last(c)

    table = [
        ("a", 0, 0), ("a", 0, 1),
        ("b", 0, 0), ("a", 1, 0),
        ("b", 0, 1), ("a", 1, 1),
        ("b", 1, 0), ("2", 0, 0),
        ("2", 0, 1), ("2", 1, 0),
        ("2", 1, 1), ("3", 0, 0),
        ("3", 0, 1), ("3", 1, 0),
        ("3", 1, 1), ("b", 1, 1),
    ]

    def off_copy(unit, p, q):
        return pltpu.make_async_copy(
            offv.at[unit, p, q], off_out.at[unit // 2, p, unit % 2, q], off_sem.at[unit, p * Q + q]
        )

    def entry(i):
        chip_z = pick(i, [zsym[name] for name, _, _ in table])
        chip_x = pick(i, [1 - x if o else x for _, o, _ in table])
        return unit_of(chip_z, chip_x, pick(i, [jnp.int32(hh) for _, _, hh in table]))

    def pieces_of(i):
        tail = i >= len(table) - 2
        unit = entry(i)
        last = [entry(jnp.int32(len(table) - 2)), entry(jnp.int32(len(table) - 1))]
        step = Q // 2
        out = []
        for k in range(2 * Q):
            out.append((
                jnp.where(tail, last[k // Q], unit),
                jnp.where(tail, k % Q // step, k // Q),
                jnp.where(tail, (i - (len(table) - 2)) * step + k % step, k % Q),
            ))
        return out

    @pl.loop(0, 8)
    def _(g):
        for k in range(1, 7):
            pl.when(g == k)(lambda k=k: phase(k))

        @pl.loop(0, 2)
        def _(j):
            i = g * 2 + j
            for t in range(2):
                pl.when(i == 14 + t)(lambda t=t: last_phase(t))
            pieces = pieces_of(i)
            rows = []
            for unit, p, q in pieces:
                start = unit // 2 * (4 * half) + p * 2 * half + unit % 2 * half + q * piece
                rows.append(lfull[pl.ds(pl.multiple_of(start, piece), piece), :])
            lt[...] = jnp.concatenate(rows, axis=0).T
            for k in range(Q):
                tail = i >= 14
                step = Q // 2
                unit, _, q = pieces[k]
                unit = jnp.where(tail, pieces[k // step * Q][0], unit)
                q = jnp.where(tail, (i - 14) * step + k % step, q)
                sub = (1 - core) * Q + q
                pltpu.make_async_copy(
                    gbuf.at[unit, sub], gbuf.at[unit, sub], recv.at[unit, sub]
                ).wait()

            @pl.loop(0, acc.shape[1] // TILE)
            def _(n):
                cols = pl.ds(pl.multiple_of(n * TILE, TILE), TILE)
                left = jnp.concatenate([gbuf[unit, p * Q + q] for unit, p, q in pieces], axis=0)
                part = jnp.dot(left, lfull[:, cols], preferred_element_type=jnp.float32)
                off = (-part).astype(jnp.bfloat16)
                for k, (unit, p, q) in enumerate(pieces):
                    offv[unit, p, q, :, cols] = off[k * piece : (k + 1) * piece]
                acc[:, cols] -= jnp.dot(lt[...], off, preferred_element_type=jnp.float32)

            for k, (unit, p, q) in enumerate(pieces):
                off_copy(unit, p, q).start()

    dv[...] = acc[...].astype(jnp.bfloat16)
    out_copy = pltpu.make_async_copy(dv, diag_out, out_sem.at[0])
    out_copy.start()

    for flag in (None, "mid", "end"):
        def drain(flag=flag):
            for when, direction, name, o, c, from_input in sent:
                if when == flag:
                    copy_of(direction, name, o, c, from_input).wait_send()

        if flag is None:
            drain()
        else:
            on(flag, drain)

    @pl.loop(0, 16)
    def _(unit):
        for p in range(2):
            for q in range(Q):
                off_copy(unit, p, q).wait()

    out_copy.wait()


def pick_kernel(struct, off_ref, diag_ref, off_out, diag_out, buf, dbuf, read_sem, write_sem):
    reads, writes = [], []
    for i in range(2):
        reads.append(pltpu.make_async_copy(diag_ref.at[i], dbuf.at[i], read_sem.at[i]))
        writes.append(pltpu.make_async_copy(dbuf.at[i], diag_out.at[i], write_sem.at[i]))
    for s in range(S):
        reads.append(pltpu.make_async_copy(off_ref.at[struct[0, s]], buf.at[s], read_sem.at[2 + s]))
        writes.append(pltpu.make_async_copy(buf.at[s], off_out.at[s], write_sem.at[2 + s]))
    for copy in reads:
        copy.start()
    for read, write in zip(reads, writes):
        read.wait()
        write.start()
    for copy in writes:
        copy.wait()


def fast(root_inverse, structure, lower_panel, diag_inverse):
    rows, width = root_inverse.shape
    depth, cols = lower_panel.shape[1:]
    piece = rows // (2 * Q)
    half = rows // 2
    chips = lax.axis_size("row") // 2
    units = 2 * chips
    bf16 = jnp.bfloat16
    dma = pltpu.SemaphoreType.DMA
    any_space = pl.BlockSpec(memory_space=pl.ANY)
    off_full, diag = pl.pallas_call(
        gather_kernel,
        out_shape=(
            jax.ShapeDtypeStruct((chips, 2, 2, Q, piece, cols), bf16),
            jax.ShapeDtypeStruct((cols, cols), bf16),
        ),
        in_specs=[any_space, pl.BlockSpec(memory_space=pltpu.SMEM), any_space, any_space],
        out_specs=(any_space, any_space),
        scratch_shapes=[
            pltpu.VMEM((units, SUB, piece, width), bf16),
            pltpu.VMEM((depth, cols), bf16),
            pltpu.VMEM((width, cols), bf16),
            pltpu.VMEM((cols, cols), jnp.float32),
            pltpu.VMEM((units, 2, Q, piece, cols), bf16),
            pltpu.VMEM((cols, cols), bf16),
            pltpu.VMEM((cols, 2 * half), bf16),
            dma((units, SUB)),
            dma((units, Q)),
            dma((units, Q)),
            dma((units, Q)),
            dma((units, Q)),
            dma((2 * Q,)),
            dma((2,)),
            dma((units, SUB)),
            dma((1,)),
        ],
        compiler_params=pltpu.CompilerParams(
            collective_id=0, has_side_effects=True, vmem_limit_bytes=56 * 1024 * 1024
        ),
        cost_estimate=pl.CostEstimate(
            flops=2 * width * cols * (width + cols), bytes_accessed=20 * 2**20, transcendentals=0
        ),
    )(root_inverse.reshape(2, Q, piece, width), structure, lower_panel[0], diag_inverse[0])
    off_full = off_full.reshape(RB, B, cols)
    off, diag = pl.pallas_call(
        pick_kernel,
        out_shape=(
            jax.ShapeDtypeStruct((S, B, cols), bf16),
            jax.ShapeDtypeStruct((2, cols // 2, cols), bf16),
        ),
        in_specs=[pl.BlockSpec(memory_space=pltpu.SMEM), any_space, any_space],
        out_specs=(any_space, any_space),
        scratch_shapes=[
            pltpu.VMEM((S, B, cols), bf16),
            pltpu.VMEM((2, cols // 2, cols), bf16),
            dma((S + 2,)),
            dma((S + 2,)),
        ],
        compiler_params=pltpu.CompilerParams(vmem_limit_bytes=60 * 1024 * 1024),
    )(structure, off_full, diag.reshape(2, cols // 2, cols))
    return off.reshape(1, depth, cols), diag.reshape(1, cols, cols)


def general(root_inverse, structure, lower_panel, diag_inverse):
    whole = lax.all_gather(root_inverse, "row", axis=0, tiled=True).reshape(RB, B, RB, B)
    offs, diags = [], []
    for child in range(structure.shape[0]):
        picked = jnp.take(whole, structure[child], axis=0)
        block = jnp.take(picked, structure[child], axis=2).reshape(S * B, S * B)
        lower = lower_panel[child]
        off = (-jnp.dot(block, lower, preferred_element_type=jnp.float32)).astype(jnp.bfloat16)
        update = lax.dot_general(
            lower, off, (((0,), (0,)), ((), ())), preferred_element_type=jnp.float32
        )
        offs.append(off)
        diags.append((diag_inverse[child].astype(jnp.float32) - update).astype(jnp.bfloat16))
    return jnp.stack(offs), jnp.stack(diags)


def solution(mesh):
    per_device = fast if mesh.shape["row"] == 16 else general
    in_specs = (
        P(("pole", "row"), None),
        P("row", None),
        P(("pole", "row"), None, None),
        P(("pole", "row"), None, None),
    )
    out_specs = (P(("pole", "row"), None, None), P(("pole", "row"), None, None))
    return jax.shard_map(
        per_device, mesh=mesh, in_specs=in_specs, out_specs=out_specs, check_vma=False
    )
```
